256 devices in a mesh: row: 32 (over x_hi, z, core), col: 8 (over y, x_lo).
Axes of the slice: x: 4 (x_hi: 2, x_lo: 2; x = x_hi * 2 + x_lo), y: 4, z: 8, core: 2. Of those that a mesh axis runs over, the one named last changes fastest.
Arguments:
- eigenvectors: float32 [65536, 4096], P('row', 'col'), may hold values from -6 to 6
- band_v0: float32 [65536, 128], P('row'), may hold values from -0.45 to 1, as said below
- band_w0: float32 [65536, 128], P('row'), may hold values from -0.15625 to 0.15625
- band_v1: float32 [65536, 128], P('row'), may hold values from -0.45 to 1, as said below
- band_w1: float32 [65536, 128], P('row'), may hold values from -0.15625 to 0.15625
- panel_y: float32 [65536, 128], P(('row', 'col')), may hold values from -0.0234375 to 0.0234375
- panel_w: float32 [65536, 128], P(('row', 'col')), may hold values from -0.25 to 0.25
Outputs:
- rotated: float32 [65536, 4096], P('row', 'col')
The draws below stay inside these ranges and needn't reach their ends.
Inputs may be any that keep to these rules, and one draw needn't show every extreme that they name: In each aligned group of 256 rows, column c of band_v0 is one at the group's row c, may be nonzero at its rows c + 1 to c + 127, and is zero elsewhere. `band_v1`: as band_v0, with groups that begin 128 rows before the aligned ones (the first one cut off at row 0).
All inputs are finite; a program needn't handle non-finite values.
Results may differ from the reference program's by a relative error of at most 0.000076.
Values sent between devices are 32-bit elements; how exact they have to be, the bound alone decides.
A program may use at most 128 MiB of HBM per device.

```python
import jax
import jax.numpy as jnp
from jax import lax

N = 65536
B = 128
K = 4096
N_COL = 8


def staircase(values, shift):
    row_index = jnp.arange(N, dtype=jnp.int32)[:, None]
    col_index = jnp.arange(B, dtype=jnp.int32)[None, :]
    within = (row_index + shift) % (2 * B)
    inside = (within > col_index) & (within < col_index + B)
    return jnp.where(within == col_index, 1.0, jnp.where(inside, values, 0.0)).astype(jnp.float32)


def draw_band_v0(key, part):
    key = jax.random.fold_in(key, 11)
    values = jnp.clip(0.09 * jax.random.normal(key, (N, B), jnp.float32), -0.45, 0.45)
    return staircase(values, 0)


def draw_band_v1(key, part):
    key = jax.random.fold_in(key, 23)
    values = jnp.clip(0.09 * jax.random.normal(key, (N, B), jnp.float32), -0.45, 0.45)
    return staircase(values, B)


def shard_levels(own_key, extent, split, low, high):
    def one(dim, blocks):
        heights = jax.random.uniform(jax.random.fold_in(jax.random.fold_in(own_key, 6), dim), (blocks,), jnp.float32, low / len(split), high / len(split))
        return jnp.repeat(jnp.exp(heights), extent[dim] // blocks).reshape((-1,) + (1,) * (len(extent) - dim - 1))

    level = one(*split[0])
    for cut in split[1:]:
        level = level * one(*cut)
    return level


def normal_values(key, shape, spread, most, cuts=(), kind=jnp.bfloat16):
    values = jax.random.normal(key, shape, jnp.float32) * spread
    if len(cuts) > 0:
        values = shard_levels(key, shape, cuts, -0.22, 0.18) * values
    return jnp.clip(values, min=-most, max=most).astype(kind)


def setup_inputs(seed: int = 0) -> dict:
    seeds = jax.random.split(jax.random.key(seed), 8)
    eigenvectors = normal_values(seeds[0], (N, K), 1.0, 6.0, ((0, 32), (1, 8)), jnp.float32)
    band_v0 = draw_band_v0(jax.random.fold_in(seeds[7], 71), 0)
    band_w0 = normal_values(seeds[2], (N, B), (12 * B) ** -0.5, 0.15625, ((0, 32),), jnp.float32)
    band_v1 = draw_band_v1(jax.random.fold_in(seeds[7], 71), 0)
    band_w1 = normal_values(seeds[4], (N, B), (12 * B) ** -0.5, 0.15625, ((0, 32),), jnp.float32)
    panel_y = normal_values(seeds[5], (N, B), N ** -0.5, 0.0234375, ((0, 256),), jnp.float32)
    panel_w = normal_values(seeds[6], (N, B), (4 * B) ** -0.5, 0.25, ((0, 256),), jnp.float32)
    return dict(eigenvectors=eigenvectors, band_v0=band_v0, band_w0=band_w0, band_v1=band_v1, band_w1=band_w1, panel_y=panel_y, panel_w=panel_w)


highest = lax.Precision.HIGHEST


def grouped(matrix, vectors, weights, height):
    groups = matrix.shape[0] // height
    blocks = matrix.reshape(groups, height, matrix.shape[1])
    vec_blocks = vectors.reshape(groups, height, vectors.shape[1])
    wt_blocks = weights.reshape(groups, height, weights.shape[1])
    projected = jnp.einsum("gik,gic->gkc", vec_blocks, blocks, precision=highest)
    update = jnp.einsum("gik,gkc->gic", wt_blocks, projected, precision=highest)
    return (blocks - update).reshape(matrix.shape)


def slab_apply(columns, band_v0, band_w0, band_v1, band_w1, panel_y, panel_w):
    after_one = grouped(columns, band_v0, band_w0, 2 * B)
    margin = jnp.zeros((B, columns.shape[1]), jnp.float32)
    padded = jnp.concatenate([margin, after_one, margin], 0)
    vectors_padded = jnp.pad(band_v1, ((B, B), (0, 0)))
    weights_padded = jnp.pad(band_w1, ((B, B), (0, 0)))
    after_two = grouped(padded, vectors_padded, weights_padded, 2 * B)[B:B + N]
    summed = jnp.einsum("ik,ic->kc", panel_y, after_two, precision=highest)
    return after_two - jnp.dot(panel_w, summed, precision=highest, preferred_element_type=jnp.float32)


def reference(eigenvectors, band_v0, band_w0, band_v1, band_w1, panel_y, panel_w):
    slab_width = K // N_COL
    pieces = [slab_apply(eigenvectors[:, offset:offset + slab_width], band_v0, band_w0, band_v1, band_w1, panel_y, panel_w) for offset in range(0, K, slab_width)]
    return jnp.concatenate(pieces, 1)
```

```python
import functools

import jax
import jax.numpy as jnp
from jax import lax
from jax.experimental import pallas as pl
from jax.experimental.pallas import tpu as pltpu
from jax.sharding import PartitionSpec as P

MESH = pl.DeviceIdType.MESH
f32, bf16 = jnp.float32, jnp.bfloat16
ROWS, COLS, B, G = 2048, 512, 128, 256
GROUPS = ROWS // G
SHARD = 256
Z, CHIPS, COL = 8, 16, 8

X, OWN_UP, OWN_DN, OTH_UP, OTH_DN, FWD_OWN_UP, FWD_OWN_DN, FWD_OTH_UP, FWD_OTH_DN = range(9)
KINDS = 9
FAR = [(1, 4), (1, 3), (1, 5), (1, 2), (1, 6), (0, 4), (1, 1), (1, 7), (0, 3), (0, 5), (1, 0), (0, 2), (0, 6), (0, 1), (0, 7)]


def split(x):
    high = x.astype(bf16)
    return high, (x - high.astype(f32)).astype(bf16)


def dot(a, b):
    return jnp.dot(a, b, preferred_element_type=f32)


def project(v, a):
    vh, vl = split(v.T)
    ah, al = split(a)
    return dot(vh, ah) + dot(vl, ah) + dot(vh, al)


def expand(w, p):
    wh, wl = split(w)
    ph, pll = split(p)
    return dot(jnp.concatenate([wh, wl], 1), jnp.concatenate([ph, ph], 0)) + dot(wh, pll)


def chain_kernel(
    e_ref, v0_ref, w0_ref, v1_ref, w1_ref, y_ref, w_ref,
    a_ref, wcat_ref, s_ref,
    v0, w0, v1, w1, ystage, yg, wg, halo_out, halo_in, total, half_out, half_in, mine, reduce_in, sums,
    in_sem, y_send, y_recv, w_send, w_recv, halo_send, halo_recv, core_send, core_recv, rs_send, rs_recv, ag_send, ag_recv,
    know_a, know_b, know_c,
):
    row, col = lax.axis_index("row"), lax.axis_index("col")
    x_hi, z, core = row // (2 * Z), (row // 2) % Z, row % 2
    chip = row // 2

    def row_of(xh, zz, cc):
        return xh * (2 * Z) + zz * 2 + cc

    def along(dx, dz):
        return ((x_hi + dx) % 2, (z + dz) % Z)

    other_col = col + 1 - 2 * (col % 2)
    up_col, down_col = (col + 2) % COL, (col + 6) % COL
    far_col = (col + 4) % COL
    to_x, to_up, to_down = (row, other_col), (row, up_col), (row, down_col)
    to_core = (row + 1 - 2 * core, col)
    next_row, prev_row = (row + 1) % (4 * Z), (row + 4 * Z - 1) % (4 * Z)
    to_next, to_prev = (next_row, col), (prev_row, col)
    to_side = (jnp.where(core == 0, prev_row, next_row), col)

    def chip_at(dx, dz):
        xh, zz = along(dx, dz)
        return (row_of(xh, zz, core), col)

    locals_ = []

    def fetch(src, dst):
        copy = pltpu.make_async_copy(src, dst, in_sem.at[len(locals_)])
        copy.start()
        locals_.append(copy)
        return copy

    get_y = fetch(y_ref, ystage)

    def part(src, dst, begin, size):
        return fetch(src.at[pl.ds(begin, size)], dst.at[pl.ds(begin, size)])

    get_e, get_edge = {}, {}
    for g in (0, GROUPS - 1):
        get_e[g] = part(e_ref, a_ref, G * g, G)
        get_edge[g] = [part(s, d, G * g, G) for s, d in ((v0_ref, v0), (w0_ref, w0), (v1_ref, v1))]

    barrier = pltpu.get_barrier_semaphore()
    near = [to_x, to_up, to_down, to_core, to_side, chip_at(0, 1), chip_at(0, Z - 1), chip_at(1, 0)]
    for device in near:
        pl.semaphore_signal(barrier, inc=1, device_id=device, device_id_type=MESH)

    inner = G * (GROUPS - 2)
    get_mid = [part(s, d, G, inner) for s, d in ((v0_ref, v0), (w0_ref, w0))]
    for g in range(1, 3):
        get_e[g] = part(e_ref, a_ref, G * g, G)
    get_mid1 = [part(s, d, G, inner) for s, d in ((v1_ref, v1), (w1_ref, w1))]
    for g in range(3, GROUPS - 1):
        get_e[g] = part(e_ref, a_ref, G * g, G)
    get_edge1 = [part(w1_ref, w1, G * g, G) for g in (0, GROUPS - 1)]
    get_w = fetch(w_ref, wg.at[pl.ds(pl.multiple_of(col * SHARD, SHARD), SHARD)])

    sent = []

    def send(src, dst, ssem, rsem, device):
        copy = pltpu.make_async_remote_copy(
            src_ref=src, dst_ref=dst, send_sem=ssem, recv_sem=rsem, device_id=device, device_id_type=MESH
        )
        copy.start()
        sent.append(copy)

    def arrived(dst, ssem, rsem):
        pltpu.make_async_remote_copy(
            src_ref=dst, dst_ref=dst, send_sem=ssem, recv_sem=rsem, device_id=to_x, device_id_type=MESH
        ).wait_recv()

    def gather(place, ssem, rsem):
        def out(kind, h, c, device):
            send(place(c, h), place(c, h), ssem.at[kind, h], rsem.at[kind, h], device)

        def wait(kind, h, c):
            arrived(place(c, h), ssem.at[kind, h], rsem.at[kind, h])

        def own():
            out(X, 0, col, to_x)
            out(OWN_UP, 0, col, to_up)
            out(OWN_DN, 1, col, to_down)
            out(X, 1, col, to_x)
            out(OWN_UP, 1, col, to_up)
            out(OWN_DN, 0, col, to_down)

        def relay(h):
            wait(X, h, other_col)
            out(OTH_UP, h, other_col, to_up)
            out(OTH_DN, h, other_col, to_down)

        def forward_own():
            wait(OWN_UP, 0, down_col)
            out(FWD_OWN_UP, 0, down_col, to_up)
            wait(OWN_DN, 1, up_col)
            out(FWD_OWN_DN, 1, up_col, to_down)

        def forward_other():
            wait(OTH_UP, 0, (other_col + 6) % COL)
            out(FWD_OTH_UP, 0, (other_col + 6) % COL, to_up)
            wait(OTH_DN, 1, (other_col + 2) % COL)
            out(FWD_OTH_DN, 1, (other_col + 2) % COL, to_down)

        def rest_own():
            wait(OWN_UP, 1, down_col)
            wait(OWN_DN, 0, up_col)

        def rest_other():
            wait(OTH_UP, 1, (other_col + 6) % COL)
            wait(OTH_DN, 0, (other_col + 2) % COL)

        def last_own():
            wait(FWD_OWN_UP, 0, far_col)
            wait(FWD_OWN_DN, 1, far_col)

        def last_other():
            wait(FWD_OTH_UP, 0, (other_col + 4) % COL)
            wait(FWD_OTH_DN, 1, (other_col + 4) % COL)

        return own, relay, forward_own, forward_other, rest_own, rest_other, last_own, last_other

    y_own, y_relay, y_fwd_own, y_fwd_oth, y_rest_own, y_rest_oth, y_last_own, y_last_oth = gather(
        lambda c, h: yg.at[c, pl.ds(64 * h, 64)], y_send, y_recv
    )
    w_own, w_relay, w_fwd_own, w_fwd_oth, w_rest_own, w_rest_oth, w_last_own, w_last_oth = gather(
        lambda c, h: wg.at[pl.ds(pl.multiple_of(c * SHARD + 128 * h, 128), 128)], w_send, w_recv
    )

    get_y.wait()
    yg[col] = ystage[...].T
    pl.semaphore_wait(barrier, len(near))
    y_own()
    for device in (chip_at(0, 1), chip_at(0, Z - 1), chip_at(1, 0)):
        pl.semaphore_signal(know_a, inc=1, device_id=device, device_id_type=MESH)

    def first(g):
        rows = pl.ds(g * G if isinstance(g, int) else pl.multiple_of(g * G, G), G)
        a = a_ref[rows, :]
        a_ref[rows, :] = a - expand(w0[rows, :], project(v0[rows, :], a))

    def second(g):
        begin = g * G + B
        rows = pl.ds(begin if isinstance(g, int) else pl.multiple_of(begin, B), G)
        a = a_ref[rows, :]
        a_ref[rows, :] = a - expand(w1[rows, :], project(v1[rows, :], a))

    top, bottom = pl.ds(0, B), pl.ds(ROWS - B, B)
    for g in (0, GROUPS - 1):
        get_e[g].wait()
        for copy in get_edge[g]:
            copy.wait()
        first(g)
        edge = top if g == 0 else bottom
        side = 0 if g == 0 else 1
        halo_out[side] = project(v1[edge, :], a_ref[edge, :])
        send(halo_out.at[side], halo_in.at[side], halo_send.at[side], halo_recv.at[side], to_prev if g == 0 else to_next)

    y_relay(0)
    for copy in get_mid:
        copy.wait()
    get_e[1].wait()
    first(1)
    y_relay(1)
    get_e[2].wait()
    first(2)
    for copy in get_mid1 + get_edge1:
        copy.wait()
    second(0)
    second(1)
    pl.semaphore_wait(know_a, 3)
    for device in (chip_at(0, 2), chip_at(0, Z - 2), chip_at(1, 0)):
        pl.semaphore_signal(know_b, inc=1, device_id=device, device_id_type=MESH)
    y_fwd_own()
    get_e[3].wait()
    get_e[4].wait()
    for g in (3, 4):
        first(g)
        second(g - 1)
    y_fwd_oth()
    get_w.wait()
    w_own()
    get_e[5].wait()
    get_e[6].wait()
    for g in (5, 6):
        first(g)
        second(g - 1)
    second(6)
    pl.semaphore_wait(know_b, 3)
    pl.semaphore_signal(know_c, inc=1, device_id=chip_at(1, 0), device_id_type=MESH)

    arrived(halo_in.at[1], halo_send.at[1], halo_recv.at[1])
    before = halo_out[0] + jnp.where(row == 0, 0.0, halo_in[1])
    a_ref[top, :] = a_ref[top, :] - expand(w1[top, :], before)
    arrived(halo_in.at[0], halo_send.at[0], halo_recv.at[0])
    after = halo_out[1] + jnp.where(row == 4 * Z - 1, 0.0, halo_in[0])
    a_ref[bottom, :] = a_ref[bottom, :] - expand(w1[bottom, :], after)

    def block(c):
        yh, yl = split(yg[c])
        ah, al = split(a_ref[pl.ds(pl.multiple_of(c * SHARD, SHARD), SHARD), :])
        return dot(yh, ah) + dot(yl, ah) + dot(yh, al)

    total[...] = block(col)
    total[...] += block(other_col)
    y_rest_own()
    total[...] += block(up_col)
    total[...] += block(down_col)
    w_relay(0)
    y_rest_oth()
    total[...] += block((other_col + 2) % COL)
    total[...] += block((other_col + 6) % COL)
    w_relay(1)
    y_last_own()
    total[...] += block(far_col)
    y_last_oth()
    total[...] += block((other_col + 4) % COL)

    half_out[...] = total[pl.ds(pl.multiple_of(64 * (1 - core), 64), 64), :]
    send(half_out, half_in, core_send.at[0], core_recv.at[0], to_core)
    pl.semaphore_wait(know_c, 1)
    arrived(half_in, core_send.at[0], core_recv.at[0])
    half = total[pl.ds(pl.multiple_of(64 * core, 64), 64), :] + half_in[...]
    for i in range(8):
        for j in range(2):
            mine[2 * i + j] = half[8 * i : 8 * i + 8, 256 * j : 256 * j + 256]
    for n, (dx, dz) in enumerate(FAR):
        xh, zz = along(dx, dz)
        send(mine.at[xh * Z + zz], reduce_in.at[n], rs_send.at[n], rs_recv.at[n], (row_of(xh, zz, core), col))
    w_fwd_own()
    for n in range(CHIPS - 1):
        arrived(reduce_in.at[n], rs_send.at[n], rs_recv.at[n])
    value = mine[chip]
    for n in range(CHIPS - 1):
        value += reduce_in[n]
    sums[core, chip] = value
    for n, (dx, dz) in enumerate(FAR):
        xh, zz = along(dx, dz)
        send(sums.at[core, chip], sums.at[core, chip], ag_send.at[n], ag_recv.at[n], (row_of(xh, zz, core), col))
    w_fwd_oth()
    w_rest_own()
    w_rest_oth()
    w_last_own()
    w_last_oth()
    for g in range(GROUPS):
        wh, wl = split(wg[pl.ds(g * G, G), :])
        wcat_ref[pl.ds(g * G, G), pl.ds(0, B)] = wh
        wcat_ref[pl.ds(g * G, G), pl.ds(B, B)] = wl
    for n, (dx, dz) in enumerate(FAR):
        xh, zz = along(dx, Z - dz)
        arrived(sums.at[core, xh * Z + zz], ag_send.at[n], ag_recv.at[n])
    send(sums.at[core], sums.at[core], core_send.at[1], core_recv.at[1], to_core)
    arrived(sums.at[1 - core], core_send.at[1], core_recv.at[1])
    for h in range(2):
        for i in range(8):
            for j in range(2):
                s_ref[pl.ds(64 * h + 8 * i, 8), pl.ds(256 * j, 256)] = sums[h, 2 * i + j]
    for copy in sent:
        copy.wait_send()


def chain(e, v0, w0, v1, w1, y, w):
    any_space = pl.BlockSpec(memory_space=pltpu.HBM)
    vmem = pl.BlockSpec(memory_space=pltpu.VMEM)
    dma = pltpu.SemaphoreType.DMA
    return pl.pallas_call(
        chain_kernel,
        out_shape=[
            pltpu.VMEM((ROWS, COLS), f32),
            pltpu.VMEM((ROWS, 2 * B), bf16),
            pltpu.VMEM((B, COLS), f32),
        ],
        in_specs=[any_space] * 7,
        out_specs=[vmem] * 3,
        scratch_shapes=[
            pltpu.VMEM((ROWS, B), f32),
            pltpu.VMEM((ROWS, B), f32),
            pltpu.VMEM((ROWS, B), f32),
            pltpu.VMEM((ROWS, B), f32),
            pltpu.VMEM((SHARD, B), f32),
            pltpu.VMEM((COL, B, SHARD), f32),
            pltpu.VMEM((ROWS, B), f32),
            pltpu.VMEM((2, B, COLS), f32),
            pltpu.VMEM((2, B, COLS), f32),
            pltpu.VMEM((B, COLS), f32),
            pltpu.VMEM((64, COLS), f32),
            pltpu.VMEM((64, COLS), f32),
            pltpu.VMEM((CHIPS, 8, 256), f32),
            pltpu.VMEM((CHIPS - 1, 8, 256), f32),
            pltpu.VMEM((2, CHIPS, 8, 256), f32),
            dma((32,)),
            dma((KINDS, 2)),
            dma((KINDS, 2)),
            dma((KINDS, 2)),
            dma((KINDS, 2)),
            dma((2,)),
            dma((2,)),
            dma((2,)),
            dma((2,)),
            dma((CHIPS - 1,)),
            dma((CHIPS - 1,)),
            dma((CHIPS - 1,)),
            dma((CHIPS - 1,)),
            pltpu.SemaphoreType.REGULAR,
            pltpu.SemaphoreType.REGULAR,
            pltpu.SemaphoreType.REGULAR,
        ],
        compiler_params=pltpu.CompilerParams(collective_id=0, has_side_effects=True, vmem_limit_bytes=40 << 20),
        name="chain",
    )(*(pltpu.with_memory_space_constraint(x, pltpu.HBM) for x in (e, v0, w0, v1, w1, y, w)))


def update_kernel(a_ref, wcat_ref, s_ref, o_ref, staged, sem):
    sh, sl = split(s_ref[...])
    twice = jnp.concatenate([sh, sh], 0)
    copies = []
    for g in range(GROUPS):
        rows = pl.ds(g * G, G)
        staged[rows, :] = a_ref[rows, :] - (dot(wcat_ref[rows, :], twice) + dot(wcat_ref[rows, :B], sl))
        copy = pltpu.make_async_copy(staged.at[rows], o_ref.at[rows], sem.at[g])
        copy.start()
        copies.append(copy)
    for copy in copies:
        copy.wait()


def update(a, wcat, s):
    a, wcat, s = (pltpu.with_memory_space_constraint(v, pltpu.VMEM) for v in (a, wcat, s))
    return pl.pallas_call(
        update_kernel,
        out_shape=jax.ShapeDtypeStruct((ROWS, COLS), f32),
        in_specs=[pl.BlockSpec(memory_space=pltpu.VMEM)] * 3,
        out_specs=pl.BlockSpec(memory_space=pl.ANY),
        scratch_shapes=[pltpu.VMEM((ROWS, COLS), f32), pltpu.SemaphoreType.DMA((GROUPS,))],
        compiler_params=pltpu.CompilerParams(vmem_limit_bytes=16 << 20),
        name="update",
    )(a, wcat, s)


def local(*operands):
    return update(*chain(*operands))


def solution(mesh):
    placed = (
        P("row", "col"),
        P("row", None),
        P("row", None),
        P("row", None),
        P("row", None),
        P(("row", "col"), None),
        P(("row", "col"), None),
    )
    return jax.shard_map(local, mesh=mesh, in_specs=placed, out_specs=P("row", "col"), check_vma=False)
```

```python
import functools

import jax
import jax.numpy as jnp
from jax import lax
from jax.experimental import pallas as pl
from jax.experimental.pallas import tpu as pltpu
from jax.sharding import PartitionSpec as P

MESH = pl.DeviceIdType.MESH
f32, bf16 = jnp.float32, jnp.bfloat16
ROWS, COLS, B, G = 2048, 512, 128, 256
GROUPS = ROWS // G
SHARD = 256
Z, CHIPS, COL = 8, 16, 8

X, FAR_Y, UP, DOWN, X_UP, X_DOWN, FAR_X = range(7)
KINDS = 7
FAR = [(1, 4), (1, 3), (1, 5), (1, 2), (1, 6), (0, 4), (1, 1), (1, 7), (0, 3), (0, 5), (1, 0), (0, 2), (0, 6), (0, 1), (0, 7)]


def split(x):
    high = x.astype(bf16)
    return high, (x - high.astype(f32)).astype(bf16)


def dot(a, b):
    return jnp.dot(a, b, preferred_element_type=f32)


def project(v, a):
    vh, vl = split(v.T)
    ah, al = split(a)
    return dot(vh, ah) + dot(vl, ah) + dot(vh, al)


def expand(w, p):
    wh, wl = split(w)
    ph, pll = split(p)
    return dot(jnp.concatenate([wh, wl], 1), jnp.concatenate([ph, ph], 0)) + dot(wh, pll)


def chain_kernel(
    e_ref, v0_ref, w0_ref, v1_ref, w1_ref, y_ref, w_ref,
    a_ref, wcat_ref, s_ref,
    v0, w0, v1, w1, ystage, yg, wg, halo_out, halo_in, total, half_out, half_in, mine, reduce_in, sums,
    in_sem, y_send, y_recv, w_send, w_recv, halo_send, halo_recv, core_send, core_recv, rs_send, rs_recv, ag_send, ag_recv,
    know_a, know_b, know_c,
):
    row, col = lax.axis_index("row"), lax.axis_index("col")
    x_hi, z, core = row // (2 * Z), (row // 2) % Z, row % 2
    chip = row // 2

    def row_of(xh, zz, cc):
        return xh * (2 * Z) + zz * 2 + cc

    def along(dx, dz):
        return ((x_hi + dx) % 2, (z + dz) % Z)

    other_col = col + 1 - 2 * (col % 2)
    up_col, down_col = (col + 2) % COL, (col + 6) % COL
    far_col = (col + 4) % COL
    to_x, to_up, to_down, to_far = (row, other_col), (row, up_col), (row, down_col), (row, far_col)
    to_core = (row + 1 - 2 * core, col)
    next_row, prev_row = (row + 1) % (4 * Z), (row + 4 * Z - 1) % (4 * Z)
    to_next, to_prev = (next_row, col), (prev_row, col)

    def chip_at(dx, dz):
        xh, zz = along(dx, dz)
        return (row_of(xh, zz, core), col)

    barrier = pltpu.get_barrier_semaphore()
    near = [to_x, to_up, to_down, to_far, to_core, chip_at(0, 1), chip_at(0, Z - 1), chip_at(1, 0)]
    for device in near:
        pl.semaphore_signal(barrier, inc=1, device_id=device, device_id_type=MESH)

    locals_ = []

    def fetch(src, dst):
        copy = pltpu.make_async_copy(src, dst, in_sem.at[len(locals_)])
        copy.start()
        locals_.append(copy)
        return copy

    get_y = fetch(y_ref, ystage)

    def part(src, dst, begin, size):
        return fetch(src.at[pl.ds(begin, size)], dst.at[pl.ds(begin, size)])

    get_e, get_edge = {}, {}
    for g in (0, GROUPS - 1):
        get_e[g] = part(e_ref, a_ref, G * g, G)
        get_edge[g] = [part(s, d, G * g, G) for s, d in ((v0_ref, v0), (w0_ref, w0), (v1_ref, v1))]

    inner = G * (GROUPS - 2)
    get_mid = [part(s, d, G, inner) for s, d in ((v0_ref, v0), (w0_ref, w0))]
    for g in range(1, 3):
        get_e[g] = part(e_ref, a_ref, G * g, G)
    get_mid1 = [part(s, d, G, inner) for s, d in ((v1_ref, v1), (w1_ref, w1))]
    for g in range(3, GROUPS - 1):
        get_e[g] = part(e_ref, a_ref, G * g, G)
    get_edge1 = [part(w1_ref, w1, G * g, G) for g in (0, GROUPS - 1)]
    get_w = fetch(w_ref, wg.at[pl.ds(pl.multiple_of(col * SHARD, SHARD), SHARD)])

    sent = []

    def send(src, dst, ssem, rsem, device):
        copy = pltpu.make_async_remote_copy(
            src_ref=src, dst_ref=dst, send_sem=ssem, recv_sem=rsem, device_id=device, device_id_type=MESH
        )
        copy.start()
        sent.append(copy)

    def arrived(dst, ssem, rsem):
        pltpu.make_async_remote_copy(
            src_ref=dst, dst_ref=dst, send_sem=ssem, recv_sem=rsem, device_id=to_x, device_id_type=MESH
        ).wait_recv()

    def gather(pieces, place, ssem, rsem):
        def out(kind, h, c, device):
            send(place(c, h), place(c, h), ssem.at[kind, h], rsem.at[kind, h], device)

        def wait(kind, h, c):
            arrived(place(c, h), ssem.at[kind, h], rsem.at[kind, h])

        def own():
            for h in range(pieces):
                out(FAR_Y, h, col, to_far)
                out(X, h, col, to_x)
            for h in range(pieces):
                out(UP, h, col, to_up)
                out(DOWN, h, col, to_down)

        def relay(h):
            wait(X, h, other_col)
            out(X_UP, h, other_col, to_up)
            out(X_DOWN, h, other_col, to_down)

        def relay_far(h):
            wait(FAR_Y, h, far_col)
            out(FAR_X, h, far_col, to_x)

        def rest_own():
            for h in range(pieces):
                wait(UP, h, down_col)
                wait(DOWN, h, up_col)

        def rest_other():
            for h in range(pieces):
                wait(X_UP, h, (other_col + 6) % COL)
                wait(X_DOWN, h, (other_col + 2) % COL)

        def rest_far():
            for h in range(pieces):
                wait(FAR_X, h, (other_col + 4) % COL)

        return own, relay, relay_far, rest_own, rest_other, rest_far

    y_own, y_relay, y_relay_far, y_rest_own, y_rest_other, y_rest_far = gather(
        2, lambda c, h: yg.at[c, pl.ds(64 * h, 64)], y_send, y_recv
    )
    w_own, w_relay, w_relay_far, w_rest_own, w_rest_other, w_rest_far = gather(
        1, lambda c, h: wg.at[pl.ds(pl.multiple_of(c * SHARD, SHARD), SHARD)], w_send, w_recv
    )

    get_y.wait()
    yg[col] = ystage[...].T
    pl.semaphore_wait(barrier, len(near))
    y_own()
    for device in (chip_at(0, 1), chip_at(0, Z - 1), chip_at(1, 0), to_core):
        pl.semaphore_signal(know_a, inc=1, device_id=device, device_id_type=MESH)

    def first(g):
        rows = pl.ds(g * G if isinstance(g, int) else pl.multiple_of(g * G, G), G)
        a = a_ref[rows, :]
        a_ref[rows, :] = a - expand(w0[rows, :], project(v0[rows, :], a))

    def second(g):
        begin = g * G + B
        rows = pl.ds(begin if isinstance(g, int) else pl.multiple_of(begin, B), G)
        a = a_ref[rows, :]
        a_ref[rows, :] = a - expand(w1[rows, :], project(v1[rows, :], a))

    top, bottom = pl.ds(0, B), pl.ds(ROWS - B, B)
    for g in (0, GROUPS - 1):
        get_e[g].wait()
        for copy in get_edge[g]:
            copy.wait()
        first(g)
        edge = top if g == 0 else bottom
        side = 0 if g == 0 else 1
        halo_out[side] = project(v1[edge, :], a_ref[edge, :])

    pl.semaphore_wait(know_a, 4)
    for device in (chip_at(0, 2), chip_at(0, Z - 2), chip_at(1, 0)):
        pl.semaphore_signal(know_b, inc=1, device_id=device, device_id_type=MESH)

    y_relay(0)
    for copy in get_mid:
        copy.wait()
    get_e[1].wait()
    first(1)
    y_relay(1)
    get_e[2].wait()
    first(2)
    for copy in get_mid1 + get_edge1:
        copy.wait()
    second(0)
    second(1)
    pl.semaphore_wait(know_b, 3)
    pl.semaphore_signal(know_c, inc=1, device_id=chip_at(1, 0), device_id_type=MESH)
    for side, device in ((0, to_prev), (1, to_next)):
        send(halo_out.at[side], halo_in.at[side], halo_send.at[side], halo_recv.at[side], device)
    y_relay_far(0)
    get_e[3].wait()
    get_e[4].wait()
    for g in (3, 4):
        first(g)
        second(g - 1)
    y_relay_far(1)
    get_w.wait()
    w_own()
    get_e[5].wait()
    get_e[6].wait()
    for g in (5, 6):
        first(g)
        second(g - 1)
    second(6)

    arrived(halo_in.at[1], halo_send.at[1], halo_recv.at[1])
    before = halo_out[0] + jnp.where(row == 0, 0.0, halo_in[1])
    a_ref[top, :] = a_ref[top, :] - expand(w1[top, :], before)
    arrived(halo_in.at[0], halo_send.at[0], halo_recv.at[0])
    after = halo_out[1] + jnp.where(row == 4 * Z - 1, 0.0, halo_in[0])
    a_ref[bottom, :] = a_ref[bottom, :] - expand(w1[bottom, :], after)

    def block(c):
        yh, yl = split(yg[c])
        ah, al = split(a_ref[pl.ds(pl.multiple_of(c * SHARD, SHARD), SHARD), :])
        return dot(yh, ah) + dot(yl, ah) + dot(yh, al)

    total[...] = block(col)
    total[...] += block(other_col)
    total[...] += block(far_col)
    y_rest_own()
    total[...] += block(up_col)
    total[...] += block(down_col)
    w_relay(0)
    y_rest_other()
    total[...] += block((other_col + 2) % COL)
    total[...] += block((other_col + 6) % COL)
    y_rest_far()
    total[...] += block((other_col + 4) % COL)

    half_out[...] = total[pl.ds(pl.multiple_of(64 * (1 - core), 64), 64), :]
    send(half_out, half_in, core_send.at[0], core_recv.at[0], to_core)
    pl.semaphore_wait(know_c, 1)
    arrived(half_in, core_send.at[0], core_recv.at[0])
    half = total[pl.ds(pl.multiple_of(64 * core, 64), 64), :] + half_in[...]
    for i in range(8):
        for j in range(2):
            mine[2 * i + j] = half[8 * i : 8 * i + 8, 256 * j : 256 * j + 256]
    for n, (dx, dz) in enumerate(FAR):
        xh, zz = along(dx, dz)
        send(mine.at[xh * Z + zz], reduce_in.at[n], rs_send.at[n], rs_recv.at[n], (row_of(xh, zz, core), col))
    w_relay_far(0)
    for n in range(CHIPS - 1):
        arrived(reduce_in.at[n], rs_send.at[n], rs_recv.at[n])
    value = mine[chip]
    for n in range(CHIPS - 1):
        value += reduce_in[n]
    sums[core, chip] = value
    for n, (dx, dz) in enumerate(FAR):
        xh, zz = along(dx, dz)
        send(sums.at[core, chip], sums.at[core, chip], ag_send.at[n], ag_recv.at[n], (row_of(xh, zz, core), col))
    w_rest_own()
    w_rest_other()
    w_rest_far()
    for g in range(GROUPS):
        wh, wl = split(wg[pl.ds(g * G, G), :])
        wcat_ref[pl.ds(g * G, G), pl.ds(0, B)] = wh
        wcat_ref[pl.ds(g * G, G), pl.ds(B, B)] = wl
    for n, (dx, dz) in enumerate(FAR):
        xh, zz = along(dx, Z - dz)
        arrived(sums.at[core, xh * Z + zz], ag_send.at[n], ag_recv.at[n])
    send(sums.at[core], sums.at[core], core_send.at[1], core_recv.at[1], to_core)
    arrived(sums.at[1 - core], core_send.at[1], core_recv.at[1])
    for h in range(2):
        for i in range(8):
            for j in range(2):
                s_ref[pl.ds(64 * h + 8 * i, 8), pl.ds(256 * j, 256)] = sums[h, 2 * i + j]
    for copy in sent:
        copy.wait_send()


def chain(e, v0, w0, v1, w1, y, w):
    any_space = pl.BlockSpec(memory_space=pltpu.HBM)
    vmem = pl.BlockSpec(memory_space=pltpu.VMEM)
    dma = pltpu.SemaphoreType.DMA
    return pl.pallas_call(
        chain_kernel,
        out_shape=[
            pltpu.VMEM((ROWS, COLS), f32),
            pltpu.VMEM((ROWS, 2 * B), bf16),
            pltpu.VMEM((B, COLS), f32),
        ],
        in_specs=[any_space] * 7,
        out_specs=[vmem] * 3,
        scratch_shapes=[
            pltpu.VMEM((ROWS, B), f32),
            pltpu.VMEM((ROWS, B), f32),
            pltpu.VMEM((ROWS, B), f32),
            pltpu.VMEM((ROWS, B), f32),
            pltpu.VMEM((SHARD, B), f32),
            pltpu.VMEM((COL, B, SHARD), f32),
            pltpu.VMEM((ROWS, B), f32),
            pltpu.VMEM((2, B, COLS), f32),
            pltpu.VMEM((2, B, COLS), f32),
            pltpu.VMEM((B, COLS), f32),
            pltpu.VMEM((64, COLS), f32),
            pltpu.VMEM((64, COLS), f32),
            pltpu.VMEM((CHIPS, 8, 256), f32),
            pltpu.VMEM((CHIPS - 1, 8, 256), f32),
            pltpu.VMEM((2, CHIPS, 8, 256), f32),
            dma((32,)),
            dma((KINDS, 2)),
            dma((KINDS, 2)),
            dma((KINDS, 2)),
            dma((KINDS, 2)),
            dma((2,)),
            dma((2,)),
            dma((2,)),
            dma((2,)),
            dma((CHIPS - 1,)),
            dma((CHIPS - 1,)),
            dma((CHIPS - 1,)),
            dma((CHIPS - 1,)),
            pltpu.SemaphoreType.REGULAR,
            pltpu.SemaphoreType.REGULAR,
            pltpu.SemaphoreType.REGULAR,
        ],
        compiler_params=pltpu.CompilerParams(collective_id=0, has_side_effects=True, vmem_limit_bytes=40 << 20),
        name="chain",
    )(*(pltpu.with_memory_space_constraint(x, pltpu.HBM) for x in (e, v0, w0, v1, w1, y, w)))


def update_kernel(a_ref, wcat_ref, s_ref, o_ref, staged, sem):
    sh, sl = split(s_ref[...])
    twice = jnp.concatenate([sh, sh], 0)
    copies = []
    for g in range(GROUPS):
        rows = pl.ds(g * G, G)
        staged[rows, :] = a_ref[rows, :] - (dot(wcat_ref[rows, :], twice) + dot(wcat_ref[rows, :B], sl))
        copy = pltpu.make_async_copy(staged.at[rows], o_ref.at[rows], sem.at[g])
        copy.start()
        copies.append(copy)
    for copy in copies:
        copy.wait()


def update(a, wcat, s):
    a, wcat, s = (pltpu.with_memory_space_constraint(v, pltpu.VMEM) for v in (a, wcat, s))
    return pl.pallas_call(
        update_kernel,
        out_shape=jax.ShapeDtypeStruct((ROWS, COLS), f32),
        in_specs=[pl.BlockSpec(memory_space=pltpu.VMEM)] * 3,
        out_specs=pl.BlockSpec(memory_space=pl.ANY),
        scratch_shapes=[pltpu.VMEM((ROWS, COLS), f32), pltpu.SemaphoreType.DMA((GROUPS,))],
        compiler_params=pltpu.CompilerParams(vmem_limit_bytes=16 << 20),
        name="update",
    )(a, wcat, s)


def local(*operands):
    return update(*chain(*operands))


def solution(mesh):
    placed = (
        P("row", "col"),
        P("row", None),
        P("row", None),
        P("row", None),
        P("row", None),
        P(("row", "col"), None),
        P(("row", "col"), None),
    )
    return jax.shard_map(local, mesh=mesh, in_specs=placed, out_specs=P("row", "col"), check_vma=False)
```

```python
import functools

import jax
import jax.numpy as jnp
from jax import lax
from jax.experimental import pallas as pl
from jax.experimental.pallas import tpu as pltpu
from jax.sharding import PartitionSpec as P

MESH = pl.DeviceIdType.MESH
f32, bf16 = jnp.float32, jnp.bfloat16
ROWS, COLS, B, G = 2048, 512, 128, 256
GROUPS = ROWS // G
SHARD = 256
Z, CHIPS, COL = 8, 16, 8

X, FAR_Y, UP, DOWN, X_UP, X_DOWN, FAR_X = range(7)
KINDS = 7
FAR = [(1, 4), (1, 3), (1, 5), (1, 2), (1, 6), (0, 4), (1, 1), (1, 7), (0, 3), (0, 5), (1, 0), (0, 2), (0, 6), (0, 1), (0, 7)]


def split(x):
    high = x.astype(bf16)
    return high, (x - high.astype(f32)).astype(bf16)


def dot(a, b):
    return jnp.dot(a, b, preferred_element_type=f32)


def thrice(x, a):
    m = x.shape[0]
    xh, xl = split(x)
    ah, al = split(a)
    both = dot(jnp.concatenate([xh, xl], 0), ah)
    return both[:m] + both[m:] + dot(xh, al)


def project(v, a):
    return thrice(v.T, a)


def expand(w, p):
    wh, wl = split(w)
    ph, pl_ = split(p)
    return dot(jnp.concatenate([wh, wl, wh], 1), jnp.concatenate([ph, ph, pl_], 0))


def chain_kernel(
    e_ref, v0_ref, w0_ref, v1_ref, w1_ref, y_ref, w_ref,
    a_ref, wcat_ref, s_ref,
    v0, w0, v1, w1, ystage, yg, wg, halo_out, halo_in, total, half_out, half_in, mine, reduce_in, sums, late_high, late_low,
    in_sem, y_send, y_recv, w_send, w_recv, halo_send, halo_recv, core_send, core_recv, rs_send, rs_recv, ag_send, ag_recv,
    know_a, know_b, know_c, know_d,
):
    row, col = lax.axis_index("row"), lax.axis_index("col")
    x_hi, z, core = row // (2 * Z), (row // 2) % Z, row % 2
    chip = row // 2

    def row_of(xh, zz, cc):
        return xh * (2 * Z) + zz * 2 + cc

    def along(dx, dz):
        return ((x_hi + dx) % 2, (z + dz) % Z)

    other_col = col + 1 - 2 * (col % 2)
    up_col, down_col = (col + 2) % COL, (col + 6) % COL
    far_col = (col + 4) % COL
    to_x, to_up, to_down, to_far = (row, other_col), (row, up_col), (row, down_col), (row, far_col)
    to_core = (row + 1 - 2 * core, col)
    next_row, prev_row = (row + 1) % (4 * Z), (row + 4 * Z - 1) % (4 * Z)
    to_side = (jnp.where(core == 0, prev_row, next_row), col)

    def chip_at(dx, dz):
        xh, zz = along(dx, dz)
        return (row_of(xh, zz, core), col)

    barrier = pltpu.get_barrier_semaphore()
    near = [to_x, to_up, to_down, to_far, to_core, chip_at(0, 1), chip_at(0, Z - 1), chip_at(1, 0)]
    for device in near:
        pl.semaphore_signal(barrier, inc=1, device_id=device, device_id_type=MESH)

    locals_ = []

    def fetch(src, dst):
        copy = pltpu.make_async_copy(src, dst, in_sem.at[len(locals_)])
        copy.start()
        locals_.append(copy)
        return copy

    get_y = fetch(y_ref, ystage)

    def part(src, dst, begin, size):
        return fetch(src.at[pl.ds(begin, size)], dst.at[pl.ds(begin, size)])

    get_e, get_edge = {}, {}
    for g in (0, GROUPS - 1):
        get_e[g] = part(e_ref, a_ref, G * g, G)
        get_edge[g] = [part(s, d, G * g, G) for s, d in ((v0_ref, v0), (w0_ref, w0), (v1_ref, v1))]

    inner = G * (GROUPS - 2)
    get_mid = [part(s, d, G, inner) for s, d in ((v0_ref, v0), (w0_ref, w0))]
    for g in range(1, 3):
        get_e[g] = part(e_ref, a_ref, G * g, G)
    get_mid1 = [part(s, d, G, inner) for s, d in ((v1_ref, v1), (w1_ref, w1))]
    for g in range(3, GROUPS - 1):
        get_e[g] = part(e_ref, a_ref, G * g, G)
    get_edge1 = [part(w1_ref, w1, G * g, G) for g in (0, GROUPS - 1)]
    get_w = fetch(w_ref, wg.at[pl.ds(pl.multiple_of(col * SHARD, SHARD), SHARD)])

    sent = []

    def send(src, dst, ssem, rsem, device):
        copy = pltpu.make_async_remote_copy(
            src_ref=src, dst_ref=dst, send_sem=ssem, recv_sem=rsem, device_id=device, device_id_type=MESH
        )
        copy.start()
        sent.append(copy)

    def arrived(dst, ssem, rsem):
        pltpu.make_async_remote_copy(
            src_ref=dst, dst_ref=dst, send_sem=ssem, recv_sem=rsem, device_id=to_x, device_id_type=MESH
        ).wait_recv()

    def gather(pieces, place, ssem, rsem):
        def out(kind, h, c, device):
            send(place(c, h), place(c, h), ssem.at[kind, h], rsem.at[kind, h], device)

        def wait(kind, h, c):
            arrived(place(c, h), ssem.at[kind, h], rsem.at[kind, h])

        def own():
            for h in range(pieces):
                out(FAR_Y, h, col, to_far)
                out(X, h, col, to_x)
            for h in range(pieces):
                out(UP, h, col, to_up)
                out(DOWN, h, col, to_down)

        def relay(h):
            wait(X, h, other_col)
            out(X_UP, h, other_col, to_up)
            out(X_DOWN, h, other_col, to_down)

        def relay_far(h):
            wait(FAR_Y, h, far_col)
            out(FAR_X, h, far_col, to_x)

        def rest_own():
            for h in range(pieces):
                wait(UP, h, down_col)
                wait(DOWN, h, up_col)

        def rest_other():
            for h in range(pieces):
                wait(X_UP, h, (other_col + 6) % COL)
                wait(X_DOWN, h, (other_col + 2) % COL)

        def rest_far():
            for h in range(pieces):
                wait(FAR_X, h, (other_col + 4) % COL)

        return own, relay, relay_far, rest_own, rest_other, rest_far

    y_own, y_relay, y_relay_far, y_rest_own, y_rest_other, y_rest_far = gather(
        2, lambda c, h: yg.at[c, pl.ds(64 * h, 64)], y_send, y_recv
    )
    w_own, w_relay, w_relay_far, w_rest_own, w_rest_other, w_rest_far = gather(
        1, lambda c, h: wg.at[pl.ds(pl.multiple_of(c * SHARD, SHARD), SHARD)], w_send, w_recv
    )

    def apply(v, w, begins):
        old = [a_ref[pl.ds(i, G), :] for i in begins]
        inner_ = [project(v[pl.ds(i, G), :], a) for i, a in zip(begins, old)]
        new = [a - expand(w[pl.ds(i, G), :], p) for i, a, p in zip(begins, old, inner_)]
        for i, a in zip(begins, new):
            a_ref[pl.ds(i, G), :] = a

    def first(*groups):
        apply(v0, w0, [g * G for g in groups])

    def second(*groups):
        apply(v1, w1, [g * G + B for g in groups])

    def send_halo(side, device):
        send(halo_out.at[side], halo_in.at[side], halo_send.at[side], halo_recv.at[side], device)

    edges = (pl.ds(0, B), pl.ds(ROWS - B, B))
    get_y.wait()
    yg[col] = ystage[...].T
    for g in (0, GROUPS - 1):
        get_e[g].wait()
        for copy in get_edge[g]:
            copy.wait()
    first(0, GROUPS - 1)
    for side in range(2):
        halo_out[side] = project(v1[edges[side], :], a_ref[edges[side], :])
    pl.semaphore_wait(barrier, len(near))
    y_own()
    for device in (chip_at(0, 1), chip_at(0, Z - 1), chip_at(1, 0)):
        pl.semaphore_signal(know_a, inc=1, device_id=device, device_id_type=MESH)
    send_halo(1 - core, to_core)
    for copy in get_mid + [get_e[1], get_e[2]]:
        copy.wait()
    first(1, 2)
    for copy in get_mid1 + get_edge1:
        copy.wait()
    second(0, 1)
    pl.semaphore_wait(know_a, 3)
    for device in (chip_at(0, 2), chip_at(0, Z - 2), chip_at(1, 0)):
        pl.semaphore_signal(know_b, inc=1, device_id=device, device_id_type=MESH)
    pl.semaphore_signal(know_d, inc=1, device_id=to_core, device_id_type=MESH)
    y_relay(0)
    pl.semaphore_wait(know_d, 1)
    send_halo(core, to_side)
    get_e[3].wait()
    get_e[4].wait()
    first(3, 4)
    y_relay(1)
    second(2, 3)
    y_relay_far(0)
    get_e[5].wait()
    get_e[6].wait()
    first(5, 6)
    y_relay_far(1)
    get_w.wait()
    w_own()
    pl.semaphore_wait(know_b, 3)
    pl.semaphore_signal(know_c, inc=1, device_id=chip_at(1, 0), device_id_type=MESH)
    second(4, 5)
    second(6)
    for side in range(2):
        a_ref[edges[side], :] -= expand(w1[edges[side], :], halo_out[side])

    def rows_of(c):
        return pl.ds(pl.multiple_of(c * SHARD, SHARD), SHARD)

    def block(c):
        return thrice(yg[c], a_ref[rows_of(c), :])

    total[...] = block(col) + block(other_col) + block(far_col)
    y_rest_own()
    total[...] += block(up_col) + block(down_col)

    for side in (1, 0):
        edge, c, offset = edges[1 - side], (COL - 1) * (1 - side), (SHARD - B) * (1 - side)
        arrived(halo_in.at[side], halo_send.at[side], halo_recv.at[side])
        other = jnp.where(row == (4 * Z - 1, 0)[side], 0.0, halo_in[side])
        a_ref[edge, :] -= expand(w1[edge, :], other)

        @pl.when((col % 2 == c % 2) | (other_col == c))
        def _():
            total[...] -= expand(thrice(yg[c, :, pl.ds(offset, B)], w1[edge, :]), other)

    late = (other_col + 4) % COL, (other_col + 2) % COL, (other_col + 6) % COL
    for i, c in enumerate(late):
        late_high[i], late_low[i] = split(a_ref[rows_of(c), :])

    halves = [pl.ds(pl.multiple_of(256 * ((z + n) % 2), 256), 256) for n in range(2)]

    def late_block(i, y, columns):
        both = dot(jnp.concatenate(y, 0), late_high[i, :, columns])
        return both[:B] + both[B:] + dot(y[0], late_low[i, :, columns])

    y_rest_far()
    y = split(yg[late[0]])
    for columns in halves:
        total[:, columns] += late_block(0, y, columns)
    y_rest_other()
    y1, y2 = split(yg[late[1]]), split(yg[late[2]])
    for n, columns in enumerate(halves):
        total[:, columns] += late_block(1, y1, columns) + late_block(2, y2, columns)
        half_out[n] = total[pl.ds(pl.multiple_of(64 * (1 - core), 64), 64), columns]
        send(half_out.at[n], half_in.at[n], core_send.at[n], core_recv.at[n], to_core)
    pl.semaphore_wait(know_c, 1)
    for n, columns in enumerate(halves):
        arrived(half_in.at[n], core_send.at[n], core_recv.at[n])
        half = total[pl.ds(pl.multiple_of(64 * core, 64), 64), columns] + half_in[n]
        for i in range(8):
            mine[2 * i + (z + n) % 2] = half[8 * i : 8 * i + 8]
        for m, (dx, dz) in enumerate(FAR):
            if dz % 2 == n:
                xh, zz = along(dx, dz)
                send(mine.at[xh * Z + zz], reduce_in.at[m], rs_send.at[m], rs_recv.at[m], chip_at(dx, dz))
    w_relay(0)
    w_relay_far(0)
    for n in range(CHIPS - 1):
        arrived(reduce_in.at[n], rs_send.at[n], rs_recv.at[n])
    value = mine[chip]
    for n in range(CHIPS - 1):
        value += reduce_in[n]
    sums[core, chip] = value
    for n, (dx, dz) in enumerate(FAR):
        send(sums.at[core, chip], sums.at[core, chip], ag_send.at[n], ag_recv.at[n], chip_at(dx, dz))
    w_rest_own()
    w_rest_far()
    w_rest_other()
    for g in range(GROUPS):
        wh, wl = split(wg[pl.ds(g * G, G), :])
        wcat_ref[pl.ds(g * G, G), pl.ds(0, B)] = wh
        wcat_ref[pl.ds(g * G, G), pl.ds(B, B)] = wl
        wcat_ref[pl.ds(g * G, G), pl.ds(2 * B, B)] = wh
    planes = [pl.ds(pl.multiple_of(Z * ((x_hi + dx) % 2), Z), Z) for dx in range(2)]
    for side in range(2):
        for n, (dx, dz) in enumerate(FAR):
            if dx == side:
                xh, zz = along(dx, Z - dz)
                arrived(sums.at[core, xh * Z + zz], ag_send.at[n], ag_recv.at[n])
        whole = sums.at[core, planes[side]]
        send(whole, whole, core_send.at[2 + side], core_recv.at[2 + side], to_core)
    for side in range(2):
        arrived(sums.at[1 - core, planes[side]], core_send.at[2 + side], core_recv.at[2 + side])
    for h in range(2):
        for i in range(8):
            for j in range(2):
                s_ref[pl.ds(64 * h + 8 * i, 8), pl.ds(256 * j, 256)] = sums[h, 2 * i + j]
    for copy in sent:
        copy.wait_send()


def chain(e, v0, w0, v1, w1, y, w):
    any_space = pl.BlockSpec(memory_space=pltpu.HBM)
    vmem = pl.BlockSpec(memory_space=pltpu.VMEM)
    dma = pltpu.SemaphoreType.DMA
    return pl.pallas_call(
        chain_kernel,
        out_shape=[
            pltpu.VMEM((ROWS, COLS), f32),
            pltpu.VMEM((ROWS, 3 * B), bf16),
            pltpu.VMEM((B, COLS), f32),
        ],
        in_specs=[any_space] * 7,
        out_specs=[vmem] * 3,
        scratch_shapes=[
            pltpu.VMEM((ROWS, B), f32),
            pltpu.VMEM((ROWS, B), f32),
            pltpu.VMEM((ROWS, B), f32),
            pltpu.VMEM((ROWS, B), f32),
            pltpu.VMEM((SHARD, B), f32),
            pltpu.VMEM((COL, B, SHARD), f32),
            pltpu.VMEM((ROWS, B), f32),
            pltpu.VMEM((2, B, COLS), f32),
            pltpu.VMEM((2, B, COLS), f32),
            pltpu.VMEM((B, COLS), f32),
            pltpu.VMEM((2, 64, 256), f32),
            pltpu.VMEM((2, 64, 256), f32),
            pltpu.VMEM((CHIPS, 8, 256), f32),
            pltpu.VMEM((CHIPS - 1, 8, 256), f32),
            pltpu.VMEM((2, CHIPS, 8, 256), f32),
            pltpu.VMEM((3, SHARD, COLS), bf16),
            pltpu.VMEM((3, SHARD, COLS), bf16),
            dma((32,)),
            dma((KINDS, 2)),
            dma((KINDS, 2)),
            dma((KINDS, 2)),
            dma((KINDS, 2)),
            dma((2,)),
            dma((2,)),
            dma((4,)),
            dma((4,)),
            dma((CHIPS - 1,)),
            dma((CHIPS - 1,)),
            dma((CHIPS - 1,)),
            dma((CHIPS - 1,)),
            pltpu.SemaphoreType.REGULAR,
            pltpu.SemaphoreType.REGULAR,
            pltpu.SemaphoreType.REGULAR,
            pltpu.SemaphoreType.REGULAR,
        ],
        compiler_params=pltpu.CompilerParams(collective_id=0, has_side_effects=True, vmem_limit_bytes=40 << 20),
        name="chain",
    )(*(pltpu.with_memory_space_constraint(x, pltpu.HBM) for x in (e, v0, w0, v1, w1, y, w)))


def update_kernel(a_ref, wcat_ref, s_ref, o_ref, staged, sem):
    sh, sl = split(s_ref[...])
    s = jnp.concatenate([sh, sh, sl], 0)
    copies = []
    for g in range(GROUPS):
        rows = pl.ds(g * G, G)
        staged[rows, :] = a_ref[rows, :] - dot(wcat_ref[rows, :], s)
        copy = pltpu.make_async_copy(staged.at[rows], o_ref.at[rows], sem.at[g])
        copy.start()
        copies.append(copy)
    for copy in copies:
        copy.wait()


def update(a, wcat, s):
    a, wcat, s = (pltpu.with_memory_space_constraint(v, pltpu.VMEM) for v in (a, wcat, s))
    return pl.pallas_call(
        update_kernel,
        out_shape=jax.ShapeDtypeStruct((ROWS, COLS), f32),
        in_specs=[pl.BlockSpec(memory_space=pltpu.VMEM)] * 3,
        out_specs=pl.BlockSpec(memory_space=pl.ANY),
        scratch_shapes=[pltpu.VMEM((ROWS, COLS), f32), pltpu.SemaphoreType.DMA((GROUPS,))],
        compiler_params=pltpu.CompilerParams(vmem_limit_bytes=16 << 20),
        name="update",
    )(a, wcat, s)


def local(*operands):
    return update(*chain(*operands))


def solution(mesh):
    placed = (
        P("row", "col"),
        P("row", None),
        P("row", None),
        P("row", None),
        P("row", None),
        P(("row", "col"), None),
        P(("row", "col"), None),
    )
    return jax.shard_map(local, mesh=mesh, in_specs=placed, out_specs=P("row", "col"), check_vma=False)
```

```python
import functools

import jax
import jax.numpy as jnp
from jax import lax
from jax.experimental import pallas as pl
from jax.experimental.pallas import tpu as pltpu
from jax.sharding import PartitionSpec as P

MESH = pl.DeviceIdType.MESH
f32, bf16 = jnp.float32, jnp.bfloat16
ROWS, COLS, B, G = 2048, 512, 128, 256
GROUPS = ROWS // G
SHARD = 256
Z, CHIPS, COL = 8, 16, 8
PARTS = 16

X, FAR_Y, UP, DOWN, X_UP, X_DOWN, FAR_X = range(7)
KINDS = 7
FAR = [(1, 4), (1, 3), (1, 5), (1, 2), (1, 6), (0, 4), (1, 1), (1, 7), (0, 3), (0, 5), (1, 0), (0, 2), (0, 6), (0, 1), (0, 7)]


def split(x):
    high = x.astype(bf16)
    return high, (x - high.astype(f32)).astype(bf16)


def dot(a, b):
    return jnp.dot(a, b, preferred_element_type=f32)


def thrice(x, a):
    m = x.shape[0]
    xh, xl = split(x)
    ah, al = split(a)
    both = dot(jnp.concatenate([xh, xl], 0), ah)
    return both[:m] + both[m:] + dot(xh, al)


def project(v, a):
    return thrice(v.T, a)


def expand(w, p):
    wh, wl = split(w)
    ph, pl_ = split(p)
    return dot(jnp.concatenate([wh, wl, wh], 1), jnp.concatenate([ph, ph, pl_], 0))


def chain_kernel(
    e_ref, v0_ref, w0_ref, v1_ref, w1_ref, y_ref, w_ref,
    a_ref, wcat_ref, s_ref,
    v0, w0, v1, w1, ystage, yg, wg, halo_out, halo_in, total, half_out, half_in, mine, reduce_in, sums, late_high, late_low,
    in_sem, y_send, y_recv, w_send, w_recv, halo_send, halo_recv, core_send, core_recv, rs_send, rs_recv, ag_send, ag_recv,
    know_a, know_b, know_c, know_d,
):
    row, col = lax.axis_index("row"), lax.axis_index("col")
    x_hi, z, core = row // (2 * Z), (row // 2) % Z, row % 2
    chip = row // 2

    def row_of(xh, zz, cc):
        return xh * (2 * Z) + zz * 2 + cc

    def along(dx, dz):
        return ((x_hi + dx) % 2, (z + dz) % Z)

    other_col = col + 1 - 2 * (col % 2)
    up_col, down_col = (col + 2) % COL, (col + 6) % COL
    far_col = (col + 4) % COL
    to_x, to_up, to_down, to_far = (row, other_col), (row, up_col), (row, down_col), (row, far_col)
    to_core = (row + 1 - 2 * core, col)
    next_row, prev_row = (row + 1) % (4 * Z), (row + 4 * Z - 1) % (4 * Z)
    to_side = (jnp.where(core == 0, prev_row, next_row), col)

    def chip_at(dx, dz):
        xh, zz = along(dx, dz)
        return (row_of(xh, zz, core), col)

    barrier = pltpu.get_barrier_semaphore()
    near = [to_x, to_up, to_down, to_far, to_core, chip_at(0, 1), chip_at(0, Z - 1), chip_at(1, 0)]
    for device in near:
        pl.semaphore_signal(barrier, inc=1, device_id=device, device_id_type=MESH)

    locals_ = []

    def fetch(src, dst):
        copy = pltpu.make_async_copy(src, dst, in_sem.at[len(locals_)])
        copy.start()
        locals_.append(copy)
        return copy

    get_y = fetch(y_ref, ystage)

    def part(src, dst, begin, size):
        return fetch(src.at[pl.ds(begin, size)], dst.at[pl.ds(begin, size)])

    get_e, get_edge = {}, {}
    for g in (0, GROUPS - 1):
        get_e[g] = part(e_ref, a_ref, G * g, G)
        get_edge[g] = [part(s, d, G * g, G) for s, d in ((v0_ref, v0), (w0_ref, w0), (v1_ref, v1))]

    inner = G * (GROUPS - 2)
    get_mid = [part(s, d, G, inner) for s, d in ((v0_ref, v0), (w0_ref, w0))]
    for g in range(1, 3):
        get_e[g] = part(e_ref, a_ref, G * g, G)
    get_mid1 = [part(s, d, G, inner) for s, d in ((v1_ref, v1), (w1_ref, w1))]
    for g in range(3, GROUPS - 1):
        get_e[g] = part(e_ref, a_ref, G * g, G)
    get_edge1 = [part(w1_ref, w1, G * g, G) for g in (0, GROUPS - 1)]
    get_w = fetch(w_ref, wg.at[pl.ds(pl.multiple_of(col * SHARD, SHARD), SHARD)])

    sent = []

    def send(src, dst, ssem, rsem, device):
        copy = pltpu.make_async_remote_copy(
            src_ref=src, dst_ref=dst, send_sem=ssem, recv_sem=rsem, device_id=device, device_id_type=MESH
        )
        copy.start()
        sent.append(copy)

    def arrived(dst, ssem, rsem):
        pltpu.make_async_remote_copy(
            src_ref=dst, dst_ref=dst, send_sem=ssem, recv_sem=rsem, device_id=to_x, device_id_type=MESH
        ).wait_recv()

    def gather(pieces, place, ssem, rsem):
        def out(kind, h, c, device):
            send(place(c, h), place(c, h), ssem.at[kind, h], rsem.at[kind, h], device)

        def wait(kind, h, c):
            arrived(place(c, h), ssem.at[kind, h], rsem.at[kind, h])

        def own():
            for h in range(pieces):
                out(FAR_Y, h, col, to_far)
                out(X, h, col, to_x)
            for h in range(pieces):
                out(UP, h, col, to_up)
                out(DOWN, h, col, to_down)

        def relay(h):
            wait(X, h, other_col)
            out(X_UP, h, other_col, to_up)
            out(X_DOWN, h, other_col, to_down)

        def relay_far(h):
            wait(FAR_Y, h, far_col)
            out(FAR_X, h, far_col, to_x)

        def rest_own():
            for h in range(pieces):
                wait(UP, h, down_col)
                wait(DOWN, h, up_col)

        def rest_other():
            for h in range(pieces):
                wait(X_UP, h, (other_col + 6) % COL)
                wait(X_DOWN, h, (other_col + 2) % COL)

        def rest_far():
            for h in range(pieces):
                wait(FAR_X, h, (other_col + 4) % COL)

        return own, relay, relay_far, rest_own, rest_other, rest_far

    y_own, y_relay, y_relay_far, y_rest_own, y_rest_other, y_rest_far = gather(
        2, lambda c, h: yg.at[c, pl.ds(64 * h, 64)], y_send, y_recv
    )
    w_own, w_relay, w_relay_far, w_rest_own, w_rest_other, w_rest_far = gather(
        1, lambda c, h: wg.at[pl.ds(pl.multiple_of(c * SHARD, SHARD), SHARD)], w_send, w_recv
    )

    def apply(v, w, begins):
        old = [a_ref[pl.ds(i, G), :] for i in begins]
        inner_ = [project(v[pl.ds(i, G), :], a) for i, a in zip(begins, old)]
        new = [a - expand(w[pl.ds(i, G), :], p) for i, a, p in zip(begins, old, inner_)]
        for i, a in zip(begins, new):
            a_ref[pl.ds(i, G), :] = a

    def first(*groups):
        apply(v0, w0, [g * G for g in groups])

    def second(*groups):
        apply(v1, w1, [g * G + B for g in groups])

    def send_halo(side, device):
        send(halo_out.at[side], halo_in.at[side], halo_send.at[side], halo_recv.at[side], device)

    edges = (pl.ds(0, B), pl.ds(ROWS - B, B))
    get_y.wait()
    yg[col] = ystage[...].T
    for g in (0, GROUPS - 1):
        get_e[g].wait()
        for copy in get_edge[g]:
            copy.wait()
    first(0, GROUPS - 1)
    for side in range(2):
        halo_out[side] = project(v1[edges[side], :], a_ref[edges[side], :])
    pl.semaphore_wait(barrier, len(near))
    y_own()
    for device in (chip_at(0, 1), chip_at(0, Z - 1), chip_at(1, 0)):
        pl.semaphore_signal(know_a, inc=1, device_id=device, device_id_type=MESH)
    send_halo(1 - core, to_core)
    for copy in get_mid + [get_e[1], get_e[2]]:
        copy.wait()
    first(1, 2)
    for copy in get_mid1 + get_edge1:
        copy.wait()
    second(0, 1)
    pl.semaphore_wait(know_a, 3)
    for device in (chip_at(0, 2), chip_at(0, Z - 2), chip_at(1, 0)):
        pl.semaphore_signal(know_b, inc=1, device_id=device, device_id_type=MESH)
    pl.semaphore_signal(know_d, inc=1, device_id=to_core, device_id_type=MESH)
    y_relay(0)
    pl.semaphore_wait(know_d, 1)
    send_halo(core, to_side)
    get_e[3].wait()
    get_e[4].wait()
    first(3, 4)
    y_relay(1)
    second(2, 3)
    y_relay_far(0)
    get_e[5].wait()
    get_e[6].wait()
    first(5, 6)
    y_relay_far(1)
    get_w.wait()
    w_own()
    pl.semaphore_wait(know_b, 3)
    pl.semaphore_signal(know_c, inc=1, device_id=chip_at(1, 0), device_id_type=MESH)
    second(4, 5)
    second(6)
    for side in range(2):
        a_ref[edges[side], :] -= expand(w1[edges[side], :], halo_out[side])

    def rows_of(c):
        return pl.ds(pl.multiple_of(c * SHARD, SHARD), SHARD)

    def block(c):
        return thrice(yg[c], a_ref[rows_of(c), :])

    total[...] = block(col) + block(other_col) + block(far_col)
    y_rest_own()
    total[...] += block(up_col) + block(down_col)

    for side in (1, 0):
        edge, c, offset = edges[1 - side], (COL - 1) * (1 - side), (SHARD - B) * (1 - side)
        arrived(halo_in.at[side], halo_send.at[side], halo_recv.at[side])
        other = jnp.where(row == (4 * Z - 1, 0)[side], 0.0, halo_in[side])
        a_ref[edge, :] -= expand(w1[edge, :], other)

        @pl.when((col % 2 == c % 2) | (other_col == c))
        def _():
            total[...] -= expand(thrice(yg[c, :, pl.ds(offset, B)], w1[edge, :]), other)

    late = (other_col + 4) % COL, (other_col + 2) % COL, (other_col + 6) % COL
    for i, c in enumerate(late):
        late_high[i], late_low[i] = split(a_ref[rows_of(c), :])

    halves = [pl.ds(pl.multiple_of(256 * ((z + n) % 2), 256), 256) for n in range(2)]

    def late_block(i, y, columns):
        both = dot(jnp.concatenate(y, 0), late_high[i, :, columns])
        return both[:B] + both[B:] + dot(y[0], late_low[i, :, columns])

    y_rest_far()
    y = split(yg[late[0]])
    for columns in halves:
        total[:, columns] += late_block(0, y, columns)
    y_rest_other()
    y1, y2 = split(yg[late[1]]), split(yg[late[2]])
    for n, columns in enumerate(halves):
        total[:, columns] += late_block(1, y1, columns) + late_block(2, y2, columns)
        half_out[n] = total[pl.ds(pl.multiple_of(64 * (1 - core), 64), 64), columns]
        send(half_out.at[n], half_in.at[n], core_send.at[n], core_recv.at[n], to_core)
    pl.semaphore_wait(know_c, 1)
    for n, columns in enumerate(halves):
        arrived(half_in.at[n], core_send.at[n], core_recv.at[n])
        half = total[pl.ds(pl.multiple_of(64 * core, 64), 64), columns] + half_in[n]
        for i in range(8):
            mine[2 * i + (z + n) % 2] = half[8 * i : 8 * i + 8]
        for m, (dx, dz) in enumerate(FAR):
            if dz % 2 == n:
                xh, zz = along(dx, dz)
                send(mine.at[xh * Z + zz], reduce_in.at[m], rs_send.at[m], rs_recv.at[m], chip_at(dx, dz))
    w_relay(0)
    w_relay_far(0)
    for n in range(CHIPS - 1):
        arrived(reduce_in.at[n], rs_send.at[n], rs_recv.at[n])
    value = mine[chip]
    for n in range(CHIPS - 1):
        value += reduce_in[n]
    sums[core, chip] = value
    for n, (dx, dz) in enumerate(FAR):
        send(sums.at[core, chip], sums.at[core, chip], ag_send.at[n], ag_recv.at[n], chip_at(dx, dz))
    w_rest_own()
    w_rest_far()
    w_rest_other()
    for g in range(GROUPS):
        wh, wl = split(wg[pl.ds(g * G, G), :])
        wcat_ref[pl.ds(g * G, G), pl.ds(0, B)] = wh
        wcat_ref[pl.ds(g * G, G), pl.ds(B, B)] = wl
        wcat_ref[pl.ds(g * G, G), pl.ds(2 * B, B)] = wh
    for copy in sent:
        copy.wait_send()
    done = len(sent)
    planes = [pl.ds(pl.multiple_of(Z * ((x_hi + dx) % 2), Z), Z) for dx in range(2)]
    for side in range(2):
        for n, (dx, dz) in enumerate(FAR):
            if dx == side:
                xh, zz = along(dx, Z - dz)
                arrived(sums.at[core, xh * Z + zz], ag_send.at[n], ag_recv.at[n])
        whole = sums.at[core, planes[side]]
        send(whole, whole, core_send.at[2 + side], core_recv.at[2 + side], to_core)
    for side in range(2):
        arrived(sums.at[1 - core, planes[side]], core_send.at[2 + side], core_recv.at[2 + side])
    for h in range(2):
        for i in range(8):
            for j in range(2):
                s_ref[pl.ds(64 * h + 8 * i, 8), pl.ds(256 * j, 256)] = sums[h, 2 * i + j]
    for copy in sent[done:]:
        copy.wait_send()


def chain(e, v0, w0, v1, w1, y, w):
    any_space = pl.BlockSpec(memory_space=pltpu.HBM)
    vmem = pl.BlockSpec(memory_space=pltpu.VMEM)
    dma = pltpu.SemaphoreType.DMA
    return pl.pallas_call(
        chain_kernel,
        out_shape=[
            pltpu.VMEM((ROWS, COLS), f32),
            pltpu.VMEM((ROWS, 3 * B), bf16),
            pltpu.VMEM((B, COLS), f32),
        ],
        in_specs=[any_space] * 7,
        out_specs=[vmem] * 3,
        scratch_shapes=[
            pltpu.VMEM((ROWS, B), f32),
            pltpu.VMEM((ROWS, B), f32),
            pltpu.VMEM((ROWS, B), f32),
            pltpu.VMEM((ROWS, B), f32),
            pltpu.VMEM((SHARD, B), f32),
            pltpu.VMEM((COL, B, SHARD), f32),
            pltpu.VMEM((ROWS, B), f32),
            pltpu.VMEM((2, B, COLS), f32),
            pltpu.VMEM((2, B, COLS), f32),
            pltpu.VMEM((B, COLS), f32),
            pltpu.VMEM((2, 64, 256), f32),
            pltpu.VMEM((2, 64, 256), f32),
            pltpu.VMEM((CHIPS, 8, 256), f32),
            pltpu.VMEM((CHIPS - 1, 8, 256), f32),
            pltpu.VMEM((2, CHIPS, 8, 256), f32),
            pltpu.VMEM((3, SHARD, COLS), bf16),
            pltpu.VMEM((3, SHARD, COLS), bf16),
            dma((32,)),
            dma((KINDS, 2)),
            dma((KINDS, 2)),
            dma((KINDS, 2)),
            dma((KINDS, 2)),
            dma((2,)),
            dma((2,)),
            dma((4,)),
            dma((4,)),
            dma((CHIPS - 1,)),
            dma((CHIPS - 1,)),
            dma((CHIPS - 1,)),
            dma((CHIPS - 1,)),
            pltpu.SemaphoreType.REGULAR,
            pltpu.SemaphoreType.REGULAR,
            pltpu.SemaphoreType.REGULAR,
            pltpu.SemaphoreType.REGULAR,
        ],
        compiler_params=pltpu.CompilerParams(collective_id=0, has_side_effects=True, vmem_limit_bytes=40 << 20),
        name="chain",
    )(*(pltpu.with_memory_space_constraint(x, pltpu.HBM) for x in (e, v0, w0, v1, w1, y, w)))


def update_kernel(a_ref, wcat_ref, s_ref, o_ref, staged, sem):
    sh, sl = split(s_ref[...])
    s = jnp.concatenate([sh, sh, sl], 0)
    copies = []
    for g in range(PARTS):
        rows = pl.ds(g * (ROWS // PARTS), ROWS // PARTS)
        staged[rows, :] = a_ref[rows, :] - dot(wcat_ref[rows, :], s)
        copy = pltpu.make_async_copy(staged.at[rows], o_ref.at[rows], sem.at[g])
        copy.start()
        copies.append(copy)
    for copy in copies:
        copy.wait()


def update(a, wcat, s):
    a, wcat, s = (pltpu.with_memory_space_constraint(v, pltpu.VMEM) for v in (a, wcat, s))
    return pl.pallas_call(
        update_kernel,
        out_shape=jax.ShapeDtypeStruct((ROWS, COLS), f32),
        in_specs=[pl.BlockSpec(memory_space=pltpu.VMEM)] * 3,
        out_specs=pl.BlockSpec(memory_space=pl.ANY),
        scratch_shapes=[pltpu.VMEM((ROWS, COLS), f32), pltpu.SemaphoreType.DMA((PARTS,))],
        compiler_params=pltpu.CompilerParams(vmem_limit_bytes=16 << 20),
        name="update",
    )(a, wcat, s)


def local(*operands):
    return update(*chain(*operands))


def solution(mesh):
    placed = (
        P("row", "col"),
        P("row", None),
        P("row", None),
        P("row", None),
        P("row", None),
        P(("row", "col"), None),
        P(("row", "col"), None),
    )
    return jax.shard_map(local, mesh=mesh, in_specs=placed, out_specs=P("row", "col"), check_vma=False)
```

```python
import functools

import jax
import jax.numpy as jnp
from jax import lax
from jax.experimental import pallas as pl
from jax.experimental.pallas import tpu as pltpu
from jax.sharding import PartitionSpec as P

MESH = pl.DeviceIdType.MESH
f32, bf16 = jnp.float32, jnp.bfloat16
ROWS, COLS, B, G = 2048, 512, 128, 256
GROUPS = ROWS // G
SHARD = 256
Z, CHIPS, COL = 8, 16, 8
PARTS = 16

X, FAR_Y, UP, DOWN, X_UP, X_DOWN, FAR_X = range(7)
KINDS = 7
FAR = [(1, 4), (1, 3), (1, 5), (1, 2), (1, 6), (0, 4), (1, 1), (1, 7), (0, 3), (0, 5), (1, 0), (0, 2), (0, 6), (0, 1), (0, 7)]


def split(x):
    high = x.astype(bf16)
    return high, (x - high.astype(f32)).astype(bf16)


def dot(a, b):
    return jnp.dot(a, b, preferred_element_type=f32)


def thrice(x, a):
    m = x.shape[0]
    xh, xl = split(x)
    ah, al = split(a)
    both = dot(jnp.concatenate([xh, xl], 0), ah)
    return both[:m] + both[m:] + dot(xh, al)


def project(v, a):
    return thrice(v.T, a)


def expand(w, p):
    wh, wl = split(w)
    ph, pl_ = split(p)
    return dot(jnp.concatenate([wh, wl, wh], 1), jnp.concatenate([ph, ph, pl_], 0))


def chain_kernel(
    e_ref, v0_ref, w0_ref, v1_ref, w1_ref, y_ref, w_ref,
    a_ref, wcat_ref, s_ref,
    v0, w0, v1, w1, ystage, yg, wg, halo_out, halo_in, total, half_out, half_in, mine, reduce_in, sums, late_high, late_low,
    in_sem, y_send, y_recv, w_send, w_recv, halo_send, halo_recv, core_send, core_recv, rs_send, rs_recv, ag_send, ag_recv,
    know_a, know_b, know_c, know_d,
):
    row, col = lax.axis_index("row"), lax.axis_index("col")
    x_hi, z, core = row // (2 * Z), (row // 2) % Z, row % 2
    chip = row // 2

    def row_of(xh, zz, cc):
        return xh * (2 * Z) + zz * 2 + cc

    def along(dx, dz):
        return ((x_hi + dx) % 2, (z + dz) % Z)

    other_col = col + 1 - 2 * (col % 2)
    up_col, down_col = (col + 2) % COL, (col + 6) % COL
    far_col = (col + 4) % COL
    to_x, to_up, to_down, to_far = (row, other_col), (row, up_col), (row, down_col), (row, far_col)
    to_core = (row + 1 - 2 * core, col)
    next_row, prev_row = (row + 1) % (4 * Z), (row + 4 * Z - 1) % (4 * Z)
    to_side = (jnp.where(core == 0, prev_row, next_row), col)

    def chip_at(dx, dz):
        xh, zz = along(dx, dz)
        return (row_of(xh, zz, core), col)

    barrier = pltpu.get_barrier_semaphore()
    near = [to_x, to_up, to_down, to_far, to_core, chip_at(0, 1), chip_at(0, Z - 1), chip_at(1, 0)]
    for device in near:
        pl.semaphore_signal(barrier, inc=1, device_id=device, device_id_type=MESH)

    locals_ = []

    def fetch(src, dst):
        copy = pltpu.make_async_copy(src, dst, in_sem.at[len(locals_)])
        copy.start()
        locals_.append(copy)
        return copy

    get_y = fetch(y_ref, ystage)

    def part(src, dst, begin, size):
        return fetch(src.at[pl.ds(begin, size)], dst.at[pl.ds(begin, size)])

    get_e, get_edge = {}, {}
    for g in (0, GROUPS - 1):
        get_e[g] = part(e_ref, a_ref, G * g, G)
        get_edge[g] = [part(s, d, G * g, G) for s, d in ((v0_ref, v0), (w0_ref, w0), (v1_ref, v1))]

    inner = G * (GROUPS - 2)
    get_mid = [part(s, d, G, inner) for s, d in ((v0_ref, v0), (w0_ref, w0))]
    for g in range(1, 3):
        get_e[g] = part(e_ref, a_ref, G * g, G)
    get_mid1 = [part(s, d, G, inner) for s, d in ((v1_ref, v1), (w1_ref, w1))]
    for g in range(3, GROUPS - 1):
        get_e[g] = part(e_ref, a_ref, G * g, G)
    get_edge1 = [part(w1_ref, w1, G * g, G) for g in (0, GROUPS - 1)]
    get_w = fetch(w_ref, wg.at[pl.ds(pl.multiple_of(col * SHARD, SHARD), SHARD)])

    sent = []

    def send(src, dst, ssem, rsem, device):
        copy = pltpu.make_async_remote_copy(
            src_ref=src, dst_ref=dst, send_sem=ssem, recv_sem=rsem, device_id=device, device_id_type=MESH
        )
        copy.start()
        sent.append(copy)

    def arrived(dst, ssem, rsem):
        pltpu.make_async_remote_copy(
            src_ref=dst, dst_ref=dst, send_sem=ssem, recv_sem=rsem, device_id=to_x, device_id_type=MESH
        ).wait_recv()

    def gather(pieces, place, ssem, rsem):
        def out(kind, h, c, device):
            send(place(c, h), place(c, h), ssem.at[kind, h], rsem.at[kind, h], device)

        def wait(kind, h, c):
            arrived(place(c, h), ssem.at[kind, h], rsem.at[kind, h])

        def own():
            for h in range(pieces):
                out(FAR_Y, h, col, to_far)
                out(X, h, col, to_x)
            for h in range(pieces):
                out(UP, h, col, to_up)
                out(DOWN, h, col, to_down)

        def relay(h):
            wait(X, h, other_col)
            out(X_UP, h, other_col, to_up)
            out(X_DOWN, h, other_col, to_down)

        def relay_far(h):
            wait(FAR_Y, h, far_col)
            out(FAR_X, h, far_col, to_x)

        def rest_own():
            for h in range(pieces):
                wait(UP, h, down_col)
                wait(DOWN, h, up_col)

        def rest_other():
            for h in range(pieces):
                wait(X_UP, h, (other_col + 6) % COL)
                wait(X_DOWN, h, (other_col + 2) % COL)

        def rest_far():
            for h in range(pieces):
                wait(FAR_X, h, (other_col + 4) % COL)

        return own, relay, relay_far, rest_own, rest_other, rest_far

    y_own, y_relay, y_relay_far, y_rest_own, y_rest_other, y_rest_far = gather(
        2, lambda c, h: yg.at[c, pl.ds(64 * h, 64)], y_send, y_recv
    )
    w_own, w_relay, w_relay_far, w_rest_own, w_rest_other, w_rest_far = gather(
        1, lambda c, h: wg.at[pl.ds(pl.multiple_of(c * SHARD, SHARD), SHARD)], w_send, w_recv
    )

    def apply(v, w, begins):
        old = [a_ref[pl.ds(i, G), :] for i in begins]
        inner_ = [project(v[pl.ds(i, G), :], a) for i, a in zip(begins, old)]
        new = [a - expand(w[pl.ds(i, G), :], p) for i, a, p in zip(begins, old, inner_)]
        for i, a in zip(begins, new):
            a_ref[pl.ds(i, G), :] = a

    def first(*groups):
        apply(v0, w0, [g * G for g in groups])

    def second(*groups):
        apply(v1, w1, [g * G + B for g in groups])

    def send_halo(side, device):
        send(halo_out.at[side], halo_in.at[side], halo_send.at[side], halo_recv.at[side], device)

    edges = (pl.ds(0, B), pl.ds(ROWS - B, B))
    get_y.wait()
    yg[col] = ystage[...].T
    for g in (0, GROUPS - 1):
        get_e[g].wait()
        for copy in get_edge[g]:
            copy.wait()
    first(0, GROUPS - 1)
    for side in range(2):
        halo_out[side] = project(v1[edges[side], :], a_ref[edges[side], :])
    pl.semaphore_wait(barrier, len(near))
    y_own()
    for device in (chip_at(0, 1), chip_at(0, Z - 1), chip_at(1, 0)):
        pl.semaphore_signal(know_a, inc=1, device_id=device, device_id_type=MESH)
    send_halo(1 - core, to_core)
    for copy in get_mid + [get_e[1], get_e[2]]:
        copy.wait()
    first(1, 2)
    for copy in get_mid1 + get_edge1:
        copy.wait()
    second(0, 1)
    pl.semaphore_wait(know_a, 3)
    for device in (chip_at(0, 2), chip_at(0, Z - 2), chip_at(1, 0)):
        pl.semaphore_signal(know_b, inc=1, device_id=device, device_id_type=MESH)
    pl.semaphore_signal(know_d, inc=1, device_id=to_core, device_id_type=MESH)
    y_relay(0)
    pl.semaphore_wait(know_d, 1)
    send_halo(core, to_side)
    get_e[3].wait()
    get_e[4].wait()
    first(3, 4)
    y_relay(1)
    second(2, 3)
    y_relay_far(0)
    get_e[5].wait()
    get_e[6].wait()
    first(5, 6)
    y_relay_far(1)
    pl.semaphore_wait(know_b, 3)
    pl.semaphore_signal(know_c, inc=1, device_id=chip_at(1, 0), device_id_type=MESH)
    second(4, 5)
    second(6)
    for side in range(2):
        a_ref[edges[side], :] -= expand(w1[edges[side], :], halo_out[side])

    def rows_of(c):
        return pl.ds(pl.multiple_of(c * SHARD, SHARD), SHARD)

    def block(c):
        return thrice(yg[c], a_ref[rows_of(c), :])

    total[...] = block(col) + block(other_col) + block(far_col)
    y_rest_own()
    total[...] += block(up_col) + block(down_col)
    get_w.wait()
    w_own()

    for side in (1, 0):
        edge, c, offset = edges[1 - side], (COL - 1) * (1 - side), (SHARD - B) * (1 - side)
        arrived(halo_in.at[side], halo_send.at[side], halo_recv.at[side])
        other = jnp.where(row == (4 * Z - 1, 0)[side], 0.0, halo_in[side])
        a_ref[edge, :] -= expand(w1[edge, :], other)

        @pl.when((col % 2 == c % 2) | (other_col == c))
        def _():
            total[...] -= expand(thrice(yg[c, :, pl.ds(offset, B)], w1[edge, :]), other)

    late = (other_col + 4) % COL, (other_col + 2) % COL, (other_col + 6) % COL
    for i, c in enumerate(late):
        late_high[i], late_low[i] = split(a_ref[rows_of(c), :])

    halves = [pl.ds(pl.multiple_of(256 * ((z + n) % 2), 256), 256) for n in range(2)]

    def late_block(i, y, columns):
        both = dot(jnp.concatenate(y, 0), late_high[i, :, columns])
        return both[:B] + both[B:] + dot(y[0], late_low[i, :, columns])

    y_rest_far()
    y = split(yg[late[0]])
    for columns in halves:
        total[:, columns] += late_block(0, y, columns)
    y_rest_other()
    y1, y2 = split(yg[late[1]]), split(yg[late[2]])
    for n, columns in enumerate(halves):
        total[:, columns] += late_block(1, y1, columns) + late_block(2, y2, columns)
        half_out[n] = total[pl.ds(pl.multiple_of(64 * (1 - core), 64), 64), columns]
        send(half_out.at[n], half_in.at[n], core_send.at[n], core_recv.at[n], to_core)
    pl.semaphore_wait(know_c, 1)
    for n, columns in enumerate(halves):
        arrived(half_in.at[n], core_send.at[n], core_recv.at[n])
        half = total[pl.ds(pl.multiple_of(64 * core, 64), 64), columns] + half_in[n]
        for i in range(8):
            mine[2 * i + (z + n) % 2] = half[8 * i : 8 * i + 8]
        for m, (dx, dz) in enumerate(FAR):
            if dz % 2 == n:
                xh, zz = along(dx, dz)
                send(mine.at[xh * Z + zz], reduce_in.at[m], rs_send.at[m], rs_recv.at[m], chip_at(dx, dz))
    w_relay(0)
    w_relay_far(0)
    for n in range(CHIPS - 1):
        arrived(reduce_in.at[n], rs_send.at[n], rs_recv.at[n])
    value = mine[chip]
    for n in range(CHIPS - 1):
        value += reduce_in[n]
    sums[core, chip] = value
    for n, (dx, dz) in enumerate(FAR):
        send(sums.at[core, chip], sums.at[core, chip], ag_send.at[n], ag_recv.at[n], chip_at(dx, dz))
    w_rest_own()
    w_rest_far()
    w_rest_other()
    for g in range(GROUPS):
        wh, wl = split(wg[pl.ds(g * G, G), :])
        wcat_ref[pl.ds(g * G, G), pl.ds(0, B)] = wh
        wcat_ref[pl.ds(g * G, G), pl.ds(B, B)] = wl
        wcat_ref[pl.ds(g * G, G), pl.ds(2 * B, B)] = wh
    for copy in sent:
        copy.wait_send()
    done = len(sent)
    planes = [pl.ds(pl.multiple_of(Z * ((x_hi + dx) % 2), Z), Z) for dx in range(2)]
    for side in range(2):
        for n, (dx, dz) in enumerate(FAR):
            if dx == side:
                xh, zz = along(dx, Z - dz)
                arrived(sums.at[core, xh * Z + zz], ag_send.at[n], ag_recv.at[n])
        whole = sums.at[core, planes[side]]
        send(whole, whole, core_send.at[2 + side], core_recv.at[2 + side], to_core)
    for side in range(2):
        arrived(sums.at[1 - core, planes[side]], core_send.at[2 + side], core_recv.at[2 + side])
    for h in range(2):
        for i in range(8):
            for j in range(2):
                s_ref[pl.ds(64 * h + 8 * i, 8), pl.ds(256 * j, 256)] = sums[h, 2 * i + j]
    for copy in sent[done:]:
        copy.wait_send()


def chain(e, v0, w0, v1, w1, y, w):
    any_space = pl.BlockSpec(memory_space=pltpu.HBM)
    vmem = pl.BlockSpec(memory_space=pltpu.VMEM)
    dma = pltpu.SemaphoreType.DMA
    return pl.pallas_call(
        chain_kernel,
        out_shape=[
            pltpu.VMEM((ROWS, COLS), f32),
            pltpu.VMEM((ROWS, 3 * B), bf16),
            pltpu.VMEM((B, COLS), f32),
        ],
        in_specs=[any_space] * 7,
        out_specs=[vmem] * 3,
        scratch_shapes=[
            pltpu.VMEM((ROWS, B), f32),
            pltpu.VMEM((ROWS, B), f32),
            pltpu.VMEM((ROWS, B), f32),
            pltpu.VMEM((ROWS, B), f32),
            pltpu.VMEM((SHARD, B), f32),
            pltpu.VMEM((COL, B, SHARD), f32),
            pltpu.VMEM((ROWS, B), f32),
            pltpu.VMEM((2, B, COLS), f32),
            pltpu.VMEM((2, B, COLS), f32),
            pltpu.VMEM((B, COLS), f32),
            pltpu.VMEM((2, 64, 256), f32),
            pltpu.VMEM((2, 64, 256), f32),
            pltpu.VMEM((CHIPS, 8, 256), f32),
            pltpu.VMEM((CHIPS - 1, 8, 256), f32),
            pltpu.VMEM((2, CHIPS, 8, 256), f32),
            pltpu.VMEM((3, SHARD, COLS), bf16),
            pltpu.VMEM((3, SHARD, COLS), bf16),
            dma((32,)),
            dma((KINDS, 2)),
            dma((KINDS, 2)),
            dma((KINDS, 2)),
            dma((KINDS, 2)),
            dma((2,)),
            dma((2,)),
            dma((4,)),
            dma((4,)),
            dma((CHIPS - 1,)),
            dma((CHIPS - 1,)),
            dma((CHIPS - 1,)),
            dma((CHIPS - 1,)),
            pltpu.SemaphoreType.REGULAR,
            pltpu.SemaphoreType.REGULAR,
            pltpu.SemaphoreType.REGULAR,
            pltpu.SemaphoreType.REGULAR,
        ],
        compiler_params=pltpu.CompilerParams(collective_id=0, has_side_effects=True, vmem_limit_bytes=40 << 20),
        name="chain",
    )(*(pltpu.with_memory_space_constraint(x, pltpu.HBM) for x in (e, v0, w0, v1, w1, y, w)))


def update_kernel(a_ref, wcat_ref, s_ref, o_ref, staged, sem):
    sh, sl = split(s_ref[...])
    s = jnp.concatenate([sh, sh, sl], 0)
    copies = []
    for g in range(PARTS):
        rows = pl.ds(g * (ROWS // PARTS), ROWS // PARTS)
        staged[rows, :] = a_ref[rows, :] - dot(wcat_ref[rows, :], s)
        copy = pltpu.make_async_copy(staged.at[rows], o_ref.at[rows], sem.at[g])
        copy.start()
        copies.append(copy)
    for copy in copies:
        copy.wait()


def update(a, wcat, s):
    a, wcat, s = (pltpu.with_memory_space_constraint(v, pltpu.VMEM) for v in (a, wcat, s))
    return pl.pallas_call(
        update_kernel,
        out_shape=jax.ShapeDtypeStruct((ROWS, COLS), f32),
        in_specs=[pl.BlockSpec(memory_space=pltpu.VMEM)] * 3,
        out_specs=pl.BlockSpec(memory_space=pl.ANY),
        scratch_shapes=[pltpu.VMEM((ROWS, COLS), f32), pltpu.SemaphoreType.DMA((PARTS,))],
        compiler_params=pltpu.CompilerParams(vmem_limit_bytes=16 << 20),
        name="update",
    )(a, wcat, s)


def local(*operands):
    return update(*chain(*operands))


def solution(mesh):
    placed = (
        P("row", "col"),
        P("row", None),
        P("row", None),
        P("row", None),
        P("row", None),
        P(("row", "col"), None),
        P(("row", "col"), None),
    )
    return jax.shard_map(local, mesh=mesh, in_specs=placed, out_specs=P("row", "col"), check_vma=False)
```
